32 devices in a mesh: section: 4 (over y, x), tensor: 4 (over z), dp: 2 (over core).
Axes of the slice: x: 2, y: 2, z: 4, core: 2. Of those that a mesh axis runs over, the one named last changes fastest.
Arguments:
- fwd_in: bfloat16 [4, 128, 4096], P('section', 'dp', 'tensor'), may hold values from -6 to 6
- back_in: bfloat16 [4, 128, 4096], P('section', 'dp', 'tensor'), may hold values from -6 to 6
- back_grad: bfloat16 [4, 128, 4096], P('section', 'dp', 'tensor'), may hold values from -6 to 6
- gain: float32 [4, 4096], P('section'), may hold values from 0.25 to 1.75
- w_query: bfloat16 [4, 4096, 4096], P('section', 'dp', 'tensor'), may hold values from -0.09375 to 0.09375
- w_out: bfloat16 [4, 4096, 4096], P('section', 'dp', 'tensor'), may hold values from -0.75 to 0.75
- neighbour_kv: bfloat16 [4, 1024, 2, 4096], P(None, ('section', 'tensor', 'dp')), may hold values from -6 to 6
- pattern: int32 [2, 2, 2], P(None, 'dp'), may hold values from 0 to 3
Outputs:
- next_in: bfloat16 [4, 128, 4096], P('section', 'dp', 'tensor')
- prev_grad: bfloat16 [4, 128, 4096], P('section', 'dp', 'tensor')
- kv_grad: bfloat16 [4, 1024, 2, 4096], P(None, ('section', 'tensor', 'dp'))
- gain_grad: float32 [4, 4096], P('section', 'tensor')
The draws below stay inside these ranges and needn't reach their ends.
Inputs may be any that keep to these rules, and one draw needn't show every extreme that they name: `pattern`: each entry numbers one of the 4 neighbour blocks of the span's own group.
All inputs are finite; a program needn't handle non-finite values.
Results may differ from the reference program's by a relative error of at most 0.012.
Values may be sent and summed in bfloat16 or wider, within the bound.
A program may use at most 64 MiB of HBM per device.

```python
import jax
import jax.numpy as jnp
from jax import lax

D = 4096
HEADS = 32
HD = 128
SPAN = 64
NBR = 2
NBR_LEN = 128
CPM = 1
INNER = 4096
NBLK_DP = 4
RB = 32
TOKENS = 128
NCH = 2
ROWS_ALL = 1024
N_SECTION = 4
N_TENSOR = 4
N_DP = 2


def draw_rows(key, salt):
    noise_key = jax.random.fold_in(key, salt)
    count = N_SECTION * TOKENS
    values = jax.random.truncated_normal(noise_key, -6.0, 6.0, (count, D), jnp.float32)
    return values.reshape(N_SECTION, TOKENS, D).astype(jnp.bfloat16)


def draw_fwd_in(key, part):
    return draw_rows(key, 11)


def draw_back_in(key, part):
    return draw_rows(key, 41)


def draw_w_query(key, part):
    noise_key = jax.random.fold_in(key, 21)
    values = jax.random.truncated_normal(noise_key, -6.0, 6.0, (N_SECTION, D, INNER), jnp.float32) * D ** (-0.5)
    return values.astype(jnp.bfloat16)


def draw_neighbour_kv(key, part):
    noise_key = jax.random.fold_in(key, 31)
    values = jax.random.truncated_normal(noise_key, -6.0, 6.0, (N_SECTION, ROWS_ALL, 2, INNER), jnp.float32)
    return values.astype(jnp.bfloat16)


def plant(result, key, least, largest):
    spot = [jax.random.randint(jax.random.fold_in(key, axis), (), 0, length) for axis, length in enumerate(result.shape)]
    widest = result.shape.index(max(result.shape))
    neighbour = spot[:widest] + [(spot[widest] + 1) % result.shape[widest]] + spot[widest + 1:]
    return result.at[tuple(spot)].set(least).at[tuple(neighbour)].set(largest)


def block_levels(rng, dims, pieces, smallest, high):
    factor_of = 1.0
    for dim, parts in pieces:
        steps = jax.random.uniform(jax.random.fold_in(jax.random.fold_in(rng, 6), dim), (parts,), jnp.float32, smallest / len(pieces), high / len(pieces))
        factor_of = factor_of * jnp.repeat(jnp.exp(steps), dims[dim] // parts).reshape((-1,) + (1,) * (len(dims) - 1 - dim))
    return factor_of


def gaussian(stream_key, extent, deviation, bound, shards=(), kind=jnp.bfloat16):
    array = jax.random.normal(stream_key, extent, jnp.float32) * deviation
    if len(shards) > 0:
        array = block_levels(stream_key, extent, shards, -0.22, 0.18) * array
    return jnp.clip(array, min=-bound, max=bound).astype(kind)


def setup_inputs(seed: int = 0) -> dict:
    arg_keys = jax.random.split(jax.random.key(seed), 9)
    return {
        "fwd_in": draw_fwd_in(jax.random.fold_in(arg_keys[8], 71), 0),
        "back_in": draw_back_in(jax.random.fold_in(arg_keys[8], 71), 0),
        "back_grad": gaussian(arg_keys[2], (N_SECTION, TOKENS, D), 1.0, 6.0, ((0, 4), (1, 2), (2, 4))),
        "gain": jnp.clip(1.0 + 0.15 * jax.random.normal(arg_keys[3], (N_SECTION, D), jnp.float32), 0.25, 1.75),
        "w_query": draw_w_query(jax.random.fold_in(arg_keys[8], 71), 0),
        "w_out": gaussian(arg_keys[5], (N_SECTION, INNER, D), 64 ** -0.5, 0.75, ((0, 4), (1, 2), (2, 4))),
        "neighbour_kv": draw_neighbour_kv(jax.random.fold_in(arg_keys[8], 71), 0),
        "pattern": plant(jax.random.randint(arg_keys[7], (2, NCH, NBR), 0, NBLK_DP), jax.random.fold_in(arg_keys[7], 1), 0, NBLK_DP - 1).astype(jnp.int32),
    }


norm_eps = 1e-05

def attend(queries, key_rows, values):
    score_scale = queries.shape[-1] ** (-0.5)
    scores = jnp.einsum('clhe,crhe->chlr', queries.astype(jnp.float32), key_rows.astype(jnp.float32)) * score_scale
    soft_probs = jax.nn.softmax(scores, axis=-1)
    rounded = lax.optimization_barrier(soft_probs.astype(jnp.bfloat16)).astype(jnp.float32)
    blended = jnp.einsum('chlr,crhe->clhe', rounded, values.astype(jnp.float32))
    return (blended.astype(jnp.bfloat16), soft_probs)

def attend_back(grad_out, soft_probs, queries, key_rows, values):
    score_scale = queries.shape[-1] ** (-0.5)
    rounded = lax.optimization_barrier(soft_probs.astype(jnp.bfloat16)).astype(jnp.float32)
    grad_wide = grad_out.astype(jnp.float32)
    grad_values = jnp.einsum('chlr,clhe->crhe', rounded, grad_wide)
    grad_probs = jnp.einsum('clhe,crhe->chlr', grad_wide, values.astype(jnp.float32))
    grad_scores = soft_probs * (grad_probs - lax.optimization_barrier(jnp.sum(grad_probs * soft_probs, axis=-1, keepdims=True)))
    scaled = lax.optimization_barrier((grad_scores * score_scale).astype(jnp.bfloat16)).astype(jnp.float32)
    grad_queries = jnp.einsum('chlr,crhe->clhe', scaled, key_rows.astype(jnp.float32)).astype(jnp.bfloat16)
    grad_keys = jnp.einsum('chlr,clhe->crhe', scaled, queries.astype(jnp.float32))
    return (grad_queries, grad_keys, grad_values)

def reference(fwd_in, back_in, back_grad, gain, w_query, w_out, neighbour_kv, pattern):
    groups = N_DP * CPM
    kv_groups = neighbour_kv.reshape(N_SECTION, N_SECTION, N_TENSOR, N_DP, RB, 2, INNER)
    kv_groups = kv_groups.transpose(0, 3, 2, 1, 4, 5, 6).reshape(N_SECTION, N_DP, NBLK_DP, NBR_LEN, 2, HEADS, HD)
    picks = pattern.reshape(2, N_DP, CPM, NBR)
    onehot = (picks[1][..., None] == jnp.arange(NBLK_DP, dtype=jnp.int32)).astype(jnp.float32)

    def neighbours(blocks, chosen):
        picked = jax.vmap(lambda group_blocks, group_picks: group_blocks[group_picks])(blocks, chosen)
        key_rows = picked[:, :, :, :, 0].reshape(groups, NBR * NBR_LEN, HEADS, HD)
        values = picked[:, :, :, :, 1].reshape(groups, NBR * NBR_LEN, HEADS, HD)
        return (key_rows, values)

    def run_layer(rows, layer_index, key_rows, values):
        wide_rows = rows.astype(jnp.float32)
        inv_rms = lax.rsqrt(lax.optimization_barrier(jnp.mean(wide_rows * wide_rows, axis=-1)) + norm_eps)
        normed = (wide_rows * inv_rms[:, None] * gain[layer_index]).astype(jnp.bfloat16)
        queries = jnp.dot(normed, w_query[layer_index], preferred_element_type=jnp.float32).astype(jnp.bfloat16)
        queries = queries.reshape(groups, SPAN, HEADS, HD)
        blended, soft_probs = attend(queries, key_rows, values)
        return (wide_rows, inv_rms, queries, blended, soft_probs)
    results = []
    grads = []
    kv_grads = []
    gain_grads = []
    for layer_index in range(N_SECTION):
        blocks = kv_groups[layer_index]
        key_rows, values = neighbours(blocks, picks[0])
        wide_rows, inv_rms, queries, blended, soft_probs = run_layer(fwd_in[layer_index], layer_index, key_rows, values)
        projected = jnp.dot(blended.reshape(TOKENS, INNER), w_out[layer_index], preferred_element_type=jnp.float32)
        results.append((wide_rows + projected).astype(jnp.bfloat16))
        key_rows, values = neighbours(blocks, picks[1])
        wide_rows, inv_rms, queries, blended, soft_probs = run_layer(back_in[layer_index], layer_index, key_rows, values)
        grad_rows = back_grad[layer_index]
        grad_blended = jnp.dot(grad_rows, w_out[layer_index].T, preferred_element_type=jnp.float32).astype(jnp.bfloat16)
        grad_blended = grad_blended.reshape(groups, SPAN, HEADS, HD)
        grad_queries, grad_keys, grad_values = attend_back(grad_blended, soft_probs, queries, key_rows, values)
        grad_normed = jnp.dot(grad_queries.reshape(TOKENS, INNER), w_query[layer_index].T, preferred_element_type=jnp.float32)
        gain_grads.append(lax.optimization_barrier(jnp.sum(grad_normed * wide_rows * inv_rms[:, None], axis=0)))
        row_total = lax.optimization_barrier(jnp.sum(grad_normed * gain[layer_index] * wide_rows, axis=-1))
        grad_wide = grad_rows.astype(jnp.float32) + gain[layer_index] * inv_rms[:, None] * grad_normed
        grad_wide = grad_wide - wide_rows * (inv_rms * inv_rms * inv_rms * row_total / D)[:, None]
        grads.append(grad_wide.astype(jnp.bfloat16))
        key_blocks = jnp.einsum('dcjb,dcjrhe->dbrhe', onehot, grad_keys.reshape(N_DP, CPM, NBR, NBR_LEN, HEADS, HD))
        value_blocks = jnp.einsum('dcjb,dcjrhe->dbrhe', onehot, grad_values.reshape(N_DP, CPM, NBR, NBR_LEN, HEADS, HD))
        kv_grads.append(jnp.stack([key_blocks, value_blocks], axis=3))
    next_in = jnp.roll(jnp.stack(results), 1, axis=0)
    stacked = jnp.stack(grads)
    prev_grad = jnp.concatenate([stacked[1:], jnp.zeros_like(stacked[:1])], axis=0)
    kv_grad = jnp.stack(kv_grads).reshape(N_SECTION, N_DP, N_TENSOR, N_SECTION, RB, 2, INNER)
    kv_grad = kv_grad.transpose(0, 3, 2, 1, 4, 5, 6).reshape(neighbour_kv.shape).astype(jnp.bfloat16)
    return (next_in, prev_grad, kv_grad, jnp.stack(gain_grads))
```

```python
import functools

import jax
import jax.numpy as jnp
from jax import lax
from jax.experimental import pallas as pl
from jax.experimental.pallas import tpu as pltpu
from jax.sharding import PartitionSpec as P

HD = 128
NBLK = 4
norm_eps = 1e-05
MESH = pl.DeviceIdType.MESH
F32 = jnp.float32
BF16 = jnp.bfloat16
TILE = 256


def dot_t(a, b):
    return lax.dot_general(a, b, (((1,), (1,)), ((), ())), preferred_element_type=F32)


def dot_0(a, b):
    return lax.dot_general(a, b, (((0,), (0,)), ((), ())), preferred_element_type=F32)


def kernel(
    S, T, N,
    pat_ref, hot_ref, fwd_ref, back_ref, grad_ref, gain_ref, wq_hbm, wo_hbm, kv_hbm,
    next_ref, prev_ref, kvg_ref, gg_ref,
    wq, wo, x, xg, bgb, kvb, kvs, hs1, hr1, qp, qr, ssp, ssr, q, qf, go,
    bl, blg, gqb, rts, rtr, hs2, hr2, pp, ppr, gp, gpr, ns, nr, ps, pr,
    w_sem, xs_sem, xr_sem, gs_sem, gr_sem, ks_sem, kr_sem, h1s_sem, h1r_sem,
    qs_sem, qr_sem, zs_sem, zr_sem, bs_sem, br_sem, gqs_sem, gqr_sem, rs_sem, rr_sem,
    h2s_sem, h2r_sem, kgs_sem, kgr_sem, pps_sem, ppr_sem, gps_sem, gpr_sem, sec_sem,
):
    s, t, d = lax.axis_index("section"), lax.axis_index("tensor"), lax.axis_index("dp")
    tok, W = fwd_ref.shape
    R = T // N
    RB = kv_hbm.shape[3]
    CH = T * S // NBLK
    heads = W // HD
    width = T * W

    def dev(os=0, ot=0, od=0):
        return (lax.rem(s + os, S), lax.rem(t + ot, T), lax.rem(d + od, N))

    pairs = [(os, ot) for ot in range(T) for os in range(S) if (os, ot) != (0, 0)]
    others = [(ot, od) for ot in range(T) for od in range(1, N)]
    barrier = pltpu.get_barrier_semaphore()
    for os, ot in pairs:
        pl.semaphore_signal(barrier, inc=1, device_id=dev(os, ot), device_id_type=MESH)
    for ot, od in others:
        pl.semaphore_signal(barrier, inc=1, device_id=dev(0, ot, od), device_id_type=MESH)

    wo_copy = pltpu.make_async_copy(wo_hbm, wo, w_sem.at[0])
    wq_copy = pltpu.make_async_copy(wq_hbm, wq, w_sem.at[1])
    wo_copy.start()
    wq_copy.start()
    x[pl.ds(0, tok)] = fwd_ref[...]
    x[pl.ds(tok, tok)] = back_ref[...]
    own = pl.ds(pl.multiple_of(d * tok, tok), tok)
    bgb[own] = grad_ref[...]
    pl.semaphore_wait(barrier, len(pairs) + len(others))

    sent = []

    def send(src, dst, ssem, rsem, device):
        copy = pltpu.make_async_remote_copy(
            src_ref=src, dst_ref=dst, send_sem=ssem, recv_sem=rsem,
            device_id=device, device_id_type=MESH,
        )
        copy.start()
        sent.append((None, copy))

    def send_or_keep(src, dst, ssem, rsem, device, here):
        copy = pltpu.make_async_remote_copy(
            src_ref=src, dst_ref=dst, send_sem=ssem, recv_sem=rsem,
            device_id=device, device_id_type=MESH,
        )

        @pl.when(here)
        def _():
            pltpu.make_async_copy(src, dst, rsem).start()

        @pl.when(jnp.logical_not(here))
        def _():
            copy.start()

        sent.append((jnp.logical_not(here), copy))

    def arrived(ref, sem):
        pltpu.make_async_copy(ref, ref, sem).wait()

    core = t // R
    part = lax.rem(t, R)
    slot = part * N + d

    def half_gather(src, dst, rows, ssem, rsem):
        at = pl.ds(pl.multiple_of(d * rows, rows), rows)
        for ot in range(T):
            tt = lax.rem(t + ot, T)
            device = (s, tt, core)
            if ot == 0:
                send_or_keep(src, dst.at[part, at], ssem.at[ot], rsem.at[slot], device, core == d)
            else:
                send(src, dst.at[part, at], ssem.at[ot], rsem.at[slot], device)

    def half_gather_wait(dst, rows, rsem):
        for i in range(R):
            for e in range(N):
                arrived(dst.at[i, pl.ds(e * rows, rows)], rsem.at[i * N + e])

    def half_scatter(src, dst, ssem, rsem):
        for i in range(R):
            for e in range(N):
                here = jnp.logical_and(R * d + i == t, d == e)
                send_or_keep(
                    src.at[i, pl.ds(e * tok, tok)], dst.at[t], ssem.at[i * N + e],
                    rsem.at[t], (s, R * d + i, e), here,
                )

    def half_scatter_wait(dst, rsem):
        for e in range(T):
            arrived(dst.at[e], rsem.at[e])

    half_gather(x, xg, 2 * tok, xs_sem, xr_sem)
    for od in range(1, N):
        send(grad_ref, bgb.at[own], gs_sem.at[od], gr_sem.at[od], dev(0, 0, od))
    chunk = t * S + s
    mine = kvb.at[chunk // CH, lax.rem(chunk, CH)]
    for os, ot in pairs:
        ss, tt, _ = dev(os, ot)
        send(kv_hbm.at[ss, tt], mine, ks_sem.at[os, ot], kr_sem.at[os, ot], (ss, tt, d))
    keep_kv = pltpu.make_async_copy(kv_hbm.at[s, t], mine, kr_sem.at[0, 0])
    keep_kv.start()

    for od in range(1, N):
        arrived(bgb.at[own], gr_sem.at[od])
    wo_copy.wait()
    for i in range(R):
        @pl.loop(0, W // TILE)
        def _(j):
            cols = pl.ds(pl.multiple_of(j * TILE, TILE), TILE)
            rows = pl.ds(pl.multiple_of(i * W + j * TILE, TILE), TILE)
            hs1[i, :, cols] = dot_t(bgb[...], wo[rows, :]).astype(BF16)
    half_scatter(hs1, hr1, h1s_sem, h1r_sem)

    wq_copy.wait()
    half_gather_wait(xg, 2 * tok, xr_sem)
    squares = None
    for i in range(R):
        wide = xg[i].astype(F32)
        term = jnp.sum(wide * wide, axis=-1, keepdims=True)
        squares = term if squares is None else squares + term
        gains = gain_ref[:, pl.ds(pl.multiple_of((d * R + i) * W, W), W)]
        xg[i] = (wide * gains).astype(BF16)
    ssp[...] = jnp.broadcast_to(squares, ssp.shape)

    @pl.loop(0, W // TILE)
    def _(j):
        cols = pl.ds(pl.multiple_of(j * TILE, TILE), TILE)
        total = None
        for i in range(R):
            term = jnp.dot(xg[i], wq[pl.ds(i * W, W), cols], preferred_element_type=F32)
            total = term if total is None else total + term
        qp[:, cols] = total

    def group(e, rows):
        return pl.ds(pl.multiple_of(e * rows, rows), rows)

    for od in range(1, N):
        e = lax.rem(d + od, N)
        send(qp.at[group(e, 2 * tok)], qr.at[od - 1], qs_sem.at[od], qr_sem.at[od], (s, t, e))
        send(ssp.at[group(e, 2 * tok)], ssr.at[od - 1], zs_sem.at[od], zr_sem.at[od], (s, t, e))
    total = qp[group(d, 2 * tok)]
    squares = ssp[group(d, 2 * tok)]
    for od in range(1, N):
        arrived(qr.at[od - 1], qr_sem.at[od])
        arrived(ssr.at[od - 1], zr_sem.at[od])
        total = total + qr[od - 1]
        squares = squares + ssr[od - 1]
    inv = lax.rsqrt(squares[:, :1] * (1.0 / width) + norm_eps)
    q[...] = (total * inv).astype(BF16)
    qf[...] = total[tok:]
    inv_back = inv[tok:]
    half_scatter_wait(hr1, h1r_sem)
    total = hr1[0].astype(F32)
    for e in range(1, T):
        total = total + hr1[e].astype(F32)
    go[...] = total.astype(BF16)

    scale = HD ** (-0.5)
    keep_kv.wait()
    for os, ot in pairs:
        arrived(mine, kr_sem.at[os, ot])

    def picked(m, kind, h):
        cols = pl.ds(h * HD, HD)
        return jnp.concatenate(
            [
                kvb[pat_ref[m * 2 + j], :, kind, :, cols].reshape(CH * RB, HD)
                for j in range(2)
            ],
            axis=0,
        )

    def softmax(scores):
        e = jnp.exp(scores - jnp.max(scores, axis=-1, keepdims=True))
        return e / jnp.sum(e, axis=-1, keepdims=True)

    for h in range(heads):
        cols = pl.ds(h * HD, HD)
        probs = softmax(dot_t(q[pl.ds(0, tok), cols], picked(0, 0, h)) * scale)
        bl[:, cols] = jnp.dot(
            probs.astype(BF16), picked(0, 1, h), preferred_element_type=F32
        ).astype(BF16)
    half_gather(bl, blg, tok, bs_sem, br_sem)

    row = jnp.zeros((tok, 1), F32)
    for h in range(heads):
        cols = pl.ds(h * HD, HD)
        keys, values = picked(1, 0, h), picked(1, 1, h)
        qh = q[pl.ds(tok, tok), cols]
        gh = go[:, cols]
        probs = softmax(dot_t(qh, keys) * scale)
        rounded = probs.astype(BF16)
        gv = dot_0(rounded, gh)
        gpr_h = dot_t(gh, values)
        gs = probs * (gpr_h - jnp.sum(gpr_h * probs, axis=-1, keepdims=True))
        scaled = (gs * scale).astype(BF16)
        gq = jnp.dot(scaled, keys, preferred_element_type=F32).astype(BF16)
        gk = dot_0(scaled, qh)
        gqb[own, cols] = gq
        row = row + jnp.sum(gq.astype(F32) * qf[:, cols], axis=-1, keepdims=True)
        half = CH * RB
        for b in range(NBLK):
            h0, h1 = hot_ref[b * 2], hot_ref[b * 2 + 1]
            for kind, g in ((0, gk), (1, gv)):
                kvs[b, :, kind, :, cols] = (
                    (g[:half] * h0 + g[half:] * h1).astype(BF16).reshape(CH, RB, HD)
                )
    rts[...] = jnp.broadcast_to(row, rts.shape)
    for od in range(1, N):
        send(gqb.at[own], gqb.at[own], gqs_sem.at[od], gqr_sem.at[od], dev(0, 0, od))
    for ot in range(1, T):
        send(rts, rtr.at[ot - 1], rs_sem.at[ot], rr_sem.at[ot], dev(0, ot, 0))

    def kv_back(os, ot):
        ss, tt, _ = dev(os, ot)
        c = tt * S + ss
        return kvs.at[c // CH, lax.rem(c, CH)], (ss, tt, d)

    def kv_send(which):
        for os, ot in which:
            src, device = kv_back(os, ot)
            send(src, kvg_ref.at[s, t], kgs_sem.at[os, ot], kgr_sem.at[os, ot], device)

    kv_send([p for p in pairs if p[1] == 0])
    keep_kvg = pltpu.make_async_copy(kv_back(0, 0)[0], kvg_ref.at[s, t], kgr_sem.at[0, 0])
    keep_kvg.start()

    for od in range(1, N):
        arrived(gqb.at[own], gqr_sem.at[od])
    for i in range(R):
        @pl.loop(0, W // TILE)
        def _(j):
            cols = pl.ds(pl.multiple_of(j * TILE, TILE), TILE)
            rows = pl.ds(pl.multiple_of(i * W + j * TILE, TILE), TILE)
            hs2[i, :, cols] = dot_t(gqb[...], wq[rows, :]).astype(BF16)
    half_scatter(hs2, hr2, h2s_sem, h2r_sem)
    kv_send([p for p in pairs if p[1] != 0])

    half_gather_wait(blg, tok, br_sem)

    @pl.loop(0, W // TILE)
    def _(j):
        cols = pl.ds(pl.multiple_of(j * TILE, TILE), TILE)
        total = None
        for i in range(R):
            term = jnp.dot(blg[i], wo[pl.ds(i * W, W), cols], preferred_element_type=F32)
            total = term if total is None else total + term
        pp[:, cols] = total

    for od in range(1, N):
        e = lax.rem(d + od, N)
        send(pp.at[group(e, tok)], ppr.at[od - 1], pps_sem.at[od], ppr_sem.at[od], (s, t, e))
    total = fwd_ref[...].astype(F32) + pp[own]
    for od in range(1, N):
        arrived(ppr.at[od - 1], ppr_sem.at[od])
        total = total + ppr[od - 1]
    ns[...] = total.astype(BF16)
    send(ns, nr, sec_sem.at[0], sec_sem.at[1], dev(1))

    for ot in range(1, T):
        arrived(rtr.at[ot - 1], rr_sem.at[ot])
        row = row + rtr[ot - 1][:, :1]
    half_scatter_wait(hr2, h2r_sem)
    gn = hr2[0].astype(F32)
    for e in range(1, T):
        gn = gn + hr2[e].astype(F32)
    back = back_ref[...].astype(F32)
    gains = gain_ref[:, pl.ds(pl.multiple_of(t * W, W), W)]
    gp[...] = jnp.sum(gn * back * inv_back, axis=0, keepdims=True)
    for od in range(1, N):
        send(gp, gpr.at[od - 1], gps_sem.at[od], gpr_sem.at[od], dev(0, 0, od))
    wide = grad_ref[...].astype(F32) + gains * inv_back * gn
    wide = wide - back * (inv_back * inv_back * inv_back * row * (1.0 / width))
    ps[...] = wide.astype(BF16)
    send(ps, pr, sec_sem.at[2], sec_sem.at[3], dev(S - 1))
    total = gp[...]
    for od in range(1, N):
        arrived(gpr.at[od - 1], gpr_sem.at[od])
        total = total + gpr[od - 1]
    gg_ref[...] = total
    arrived(nr, sec_sem.at[1])
    next_ref[...] = nr[...]
    arrived(pr, sec_sem.at[3])
    keep = jnp.where(s < S - 1, 1.0, 0.0).astype(F32)
    prev_ref[...] = (pr[...].astype(F32) * keep).astype(BF16)
    keep_kvg.wait()
    for os, ot in pairs:
        arrived(kvs.at[0, 0], kgr_sem.at[os, ot])
    for cond, copy in sent:
        if cond is None:
            copy.wait_send()
        else:
            pl.when(cond)(copy.wait_send)


def on_device(S, T, N, fwd_in, back_in, back_grad, gain, w_query, w_out, neighbour_kv, pattern):
    _, tok, W = fwd_in.shape
    rb = neighbour_kv.shape[1]
    D = gain.shape[1]
    half = w_query.shape[1]
    R = T // N
    CH = T * S // NBLK
    kv = neighbour_kv.reshape(S, rb, 2, T, W).transpose(0, 3, 2, 1, 4)
    picks = pattern.reshape(4)
    hot = (picks[2:][None, :] == jnp.arange(NBLK, dtype=jnp.int32)[:, None]).astype(F32).reshape(-1)
    vm = pl.BlockSpec(memory_space=pltpu.VMEM)
    sm = pl.BlockSpec(memory_space=pltpu.SMEM)
    hb = pl.BlockSpec(memory_space=pl.ANY)
    V = pltpu.VMEM
    dma = lambda *n: pltpu.SemaphoreType.DMA(n)
    M = max(N - 1, 1)
    scratch = [
        V((half, W), BF16), V((half, W), BF16),
        V((2 * tok, W), BF16), V((R, N * 2 * tok, W), BF16), V((N * tok, W), BF16),
        V((NBLK, CH, 2, rb, W), BF16), V((NBLK, CH, 2, rb, W), BF16),
        V((R, N * tok, W), BF16), V((T, tok, W), BF16),
        V((N * 2 * tok, W), F32), V((M, 2 * tok, W), F32),
        V((N * 2 * tok, 128), F32), V((M, 2 * tok, 128), F32),
        V((2 * tok, W), BF16), V((tok, W), F32), V((tok, W), BF16),
        V((tok, W), BF16), V((R, N * tok, W), BF16), V((N * tok, W), BF16),
        V((tok, 128), F32), V((T - 1, tok, 128), F32),
        V((R, N * tok, W), BF16), V((T, tok, W), BF16),
        V((N * tok, W), F32), V((M, tok, W), F32),
        V((1, W), F32), V((M, 1, W), F32),
        V((tok, W), BF16), V((tok, W), BF16), V((tok, W), BF16), V((tok, W), BF16),
        dma(2), dma(T), dma(R * N), dma(N), dma(N), dma(S, T), dma(S, T), dma(R * N), dma(T),
        dma(N), dma(N), dma(N), dma(N), dma(T), dma(R * N), dma(N), dma(N), dma(T), dma(T),
        dma(R * N), dma(T), dma(S, T), dma(S, T), dma(N), dma(N), dma(N), dma(N), dma(4),
    ]
    next_in, prev_grad, kvg, gg = pl.pallas_call(
        functools.partial(kernel, S, T, N),
        out_shape=[
            jax.ShapeDtypeStruct((tok, W), BF16),
            jax.ShapeDtypeStruct((tok, W), BF16),
            jax.ShapeDtypeStruct((S, T, 2, rb, W), BF16),
            jax.ShapeDtypeStruct((1, W), F32),
        ],
        in_specs=[sm, sm, vm, vm, vm, vm, hb, hb, hb],
        out_specs=[vm, vm, hb, vm],
        scratch_shapes=scratch,
        compiler_params=pltpu.CompilerParams(
            collective_id=0, has_side_effects=True, vmem_limit_bytes=48 * 2**20
        ),
        cost_estimate=pl.CostEstimate(
            flops=5 * 10**9, bytes_accessed=14 * 2**20, transcendentals=2 * 10**5
        ),
    )(picks, hot, fwd_in[0], back_in[0], back_grad[0], gain, w_query[0], w_out[0], kv)
    kv_grad = kvg.transpose(0, 3, 2, 1, 4).reshape(S, rb, 2, D)
    return (next_in[None], prev_grad[None], kv_grad, gg)


def solution(mesh):
    S, T, N = (mesh.shape[a] for a in ("section", "tensor", "dp"))
    return jax.shard_map(
        functools.partial(on_device, S, T, N),
        mesh=mesh,
        in_specs=(
            P("section", "dp", "tensor"),
            P("section", "dp", "tensor"),
            P("section", "dp", "tensor"),
            P("section", None),
            P("section", "dp", "tensor"),
            P("section", "dp", "tensor"),
            P(None, ("section", "tensor", "dp"), None, None),
            P(None, "dp", None),
        ),
        out_specs=(
            P("section", "dp", "tensor"),
            P("section", "dp", "tensor"),
            P(None, ("section", "tensor", "dp"), None, None),
            P("section", "tensor"),
        ),
        check_vma=False,
    )
```

```python
import functools

import jax
import jax.numpy as jnp
from jax import lax
from jax.experimental import pallas as pl
from jax.experimental.pallas import tpu as pltpu
from jax.sharding import PartitionSpec as P

HD = 128
NBLK = 4
norm_eps = 1e-05
MESH = pl.DeviceIdType.MESH
F32 = jnp.float32
BF16 = jnp.bfloat16
TILE = 256


def dot_t(a, b):
    return lax.dot_general(a, b, (((1,), (1,)), ((), ())), preferred_element_type=F32)


def dot_0(a, b):
    return lax.dot_general(a, b, (((0,), (0,)), ((), ())), preferred_element_type=F32)


def kernel(
    S, T, N,
    pat_ref, fwd_ref, back_ref, grad_ref, gain_ref, wq_hbm, wo_hbm, kv_hbm,
    next_ref, prev_ref, kvg_ref, gg_ref,
    wq, wo, x, xg, bgb, kvb, kvs, hs1, hr1, qp, qr, ssp, ssr, q, qf, go,
    bl, blg, gqb, rts, rtr, hs2, hr2, qa, ga, ebuf, gbuf, obuf, st, sr, obs, obr, gqs, gqp, pp, ppr, gp, gpr, ns, nr, ps, pr,
    w_sem, xs_sem, xr_sem, gs_sem, gr_sem, ks_sem, kr_sem, h1s_sem, h1r_sem,
    qs_sem, qr_sem, zs_sem, zr_sem, bs_sem, br_sem, gqs_sem, gqr_sem, rs_sem, rr_sem,
    h2s_sem, h2r_sem, kgs_sem, kgr_sem, pps_sem, ppr_sem, gps_sem, gpr_sem, sec_sem,
    qas_sem, qar_sem, gas_sem, gar_sem, sts_sem, str_sem, obs_sem, obr_sem, gqps_sem, gqpr_sem,
):
    s, t, d = lax.axis_index("section"), lax.axis_index("tensor"), lax.axis_index("dp")
    tok, W = fwd_ref.shape
    R = T // N
    RB = kv_hbm.shape[2]
    heads = W // HD
    H = T * heads
    rows_here = S * RB
    width = T * W

    def dev(os=0, ot=0, od=0):
        return (lax.rem(s + os, S), lax.rem(t + ot, T), lax.rem(d + od, N))

    pairs = list(range(1, S))
    others = [(ot, od) for ot in range(T) for od in range(N) if (ot, od) != (0, 0)]
    barrier = pltpu.get_barrier_semaphore()
    for os in pairs:
        pl.semaphore_signal(barrier, inc=1, device_id=dev(os), device_id_type=MESH)
    for ot, od in others:
        pl.semaphore_signal(barrier, inc=1, device_id=dev(0, ot, od), device_id_type=MESH)

    wo_copy = pltpu.make_async_copy(wo_hbm, wo, w_sem.at[0])
    wq_copy = pltpu.make_async_copy(wq_hbm, wq, w_sem.at[1])
    wo_copy.start()
    wq_copy.start()
    x[pl.ds(0, tok)] = fwd_ref[...]
    x[pl.ds(tok, tok)] = back_ref[...]
    own = pl.ds(pl.multiple_of(d * tok, tok), tok)
    bgb[own] = grad_ref[...]
    pl.semaphore_wait(barrier, len(pairs) + len(others))

    sent = []

    def send(src, dst, ssem, rsem, device):
        copy = pltpu.make_async_remote_copy(
            src_ref=src, dst_ref=dst, send_sem=ssem, recv_sem=rsem,
            device_id=device, device_id_type=MESH,
        )
        copy.start()
        sent.append((None, copy))

    def send_or_keep(src, dst, ssem, rsem, device, here):
        copy = pltpu.make_async_remote_copy(
            src_ref=src, dst_ref=dst, send_sem=ssem, recv_sem=rsem,
            device_id=device, device_id_type=MESH,
        )

        @pl.when(here)
        def _():
            pltpu.make_async_copy(src, dst, rsem).start()

        @pl.when(jnp.logical_not(here))
        def _():
            copy.start()

        sent.append((jnp.logical_not(here), copy))

    def arrived(ref, sem):
        pltpu.make_async_copy(ref, ref, sem).wait()

    core = t // R
    part = lax.rem(t, R)
    slot = part * N + d

    def half_gather(src, dst, rows, ssem, rsem):
        at = pl.ds(pl.multiple_of(d * rows, rows), rows)
        for ot in range(T):
            tt = lax.rem(t + ot, T)
            device = (s, tt, core)
            if ot == 0:
                send_or_keep(src, dst.at[part, at], ssem.at[ot], rsem.at[slot], device, core == d)
            else:
                send(src, dst.at[part, at], ssem.at[ot], rsem.at[slot], device)

    def half_gather_wait(dst, rows, rsem):
        for i in range(R):
            for e in range(N):
                arrived(dst.at[i, pl.ds(e * rows, rows)], rsem.at[i * N + e])

    def half_scatter(src, dst, ssem, rsem):
        for i in range(R):
            for e in range(N):
                here = jnp.logical_and(R * d + i == t, d == e)
                send_or_keep(
                    src.at[i, pl.ds(e * tok, tok)], dst.at[t], ssem.at[i * N + e],
                    rsem.at[t], (s, R * d + i, e), here,
                )

    def half_scatter_wait(dst, rsem):
        for e in range(T):
            arrived(dst.at[e], rsem.at[e])

    half_gather(x, xg, 2 * tok, xs_sem, xr_sem)
    for od in range(1, N):
        send(grad_ref, bgb.at[own], gs_sem.at[od], gr_sem.at[od], dev(0, 0, od))
    for os in pairs:
        ss, _, _ = dev(os)
        send(kv_hbm.at[ss], kvb.at[s], ks_sem.at[os], kr_sem.at[os], dev(os))
    keep_kv = pltpu.make_async_copy(kv_hbm.at[s], kvb.at[s], kr_sem.at[0])
    keep_kv.start()

    for od in range(1, N):
        arrived(bgb.at[own], gr_sem.at[od])
    wo_copy.wait()
    for i in range(R):
        @pl.loop(0, W // TILE)
        def _(j):
            cols = pl.ds(pl.multiple_of(j * TILE, TILE), TILE)
            rows = pl.ds(pl.multiple_of(i * W + j * TILE, TILE), TILE)
            hs1[i, :, cols] = dot_t(bgb[...], wo[rows, :]).astype(BF16)
    half_scatter(hs1, hr1, h1s_sem, h1r_sem)

    wq_copy.wait()
    half_gather_wait(xg, 2 * tok, xr_sem)
    squares = None
    for i in range(R):
        wide = xg[i].astype(F32)
        term = jnp.sum(wide * wide, axis=-1, keepdims=True)
        squares = term if squares is None else squares + term
        gains = gain_ref[:, pl.ds(pl.multiple_of((d * R + i) * W, W), W)]
        xg[i] = (wide * gains).astype(BF16)
    ssp[...] = jnp.broadcast_to(squares, ssp.shape)

    @pl.loop(0, W // TILE)
    def _(j):
        cols = pl.ds(pl.multiple_of(j * TILE, TILE), TILE)
        total = None
        for i in range(R):
            term = jnp.dot(xg[i], wq[pl.ds(i * W, W), cols], preferred_element_type=F32)
            total = term if total is None else total + term
        qp[:, cols] = total

    def group(e, rows):
        return pl.ds(pl.multiple_of(e * rows, rows), rows)

    for od in range(1, N):
        e = lax.rem(d + od, N)
        send(qp.at[group(e, 2 * tok)], qr.at[od - 1], qs_sem.at[od], qr_sem.at[od], (s, t, e))
        send(ssp.at[group(e, 2 * tok)], ssr.at[od - 1], zs_sem.at[od], zr_sem.at[od], (s, t, e))
    total = qp[group(d, 2 * tok)]
    squares = ssp[group(d, 2 * tok)]
    for od in range(1, N):
        arrived(qr.at[od - 1], qr_sem.at[od])
        arrived(ssr.at[od - 1], zr_sem.at[od])
        total = total + qr[od - 1]
        squares = squares + ssr[od - 1]
    inv = lax.rsqrt(squares[:, :1] * (1.0 / width) + norm_eps)
    q[...] = (total * inv).astype(BF16)
    qf[...] = total[tok:]
    inv_back = inv[tok:]
    qa[0] = q[...]
    for ot in range(1, T):
        send(q, qa.at[ot], qas_sem.at[ot], qar_sem.at[ot], dev(0, ot))
    half_scatter_wait(hr1, h1r_sem)
    total = hr1[0].astype(F32)
    for e in range(1, T):
        total = total + hr1[e].astype(F32)
    go[...] = total.astype(BF16)
    ga[0] = go[...]
    for ot in range(1, T):
        send(go, ga.at[ot], gas_sem.at[ot], gar_sem.at[ot], dev(0, ot))

    scale = HD ** (-0.5)
    block = t * NBLK // T
    counts = []
    for m in range(2):
        count = jnp.float32(0.0)
        for j in range(2):
            count = count + jnp.where(pat_ref[m * 2 + j] == block, 1.0, 0.0).astype(F32)
        counts.append(count)
    is_fwd = lax.broadcasted_iota(jnp.int32, (2 * tok, 1), 0) < tok
    times = jnp.where(is_fwd, counts[0], counts[1])
    lane = lax.broadcasted_iota(jnp.int32, (2 * tok, 128), 1)
    keep_kv.wait()
    for os in pairs:
        arrived(kvb.at[s], kr_sem.at[os])

    def kv_rows(kind, cols):
        return kvb[:, kind, :, cols].reshape(rows_here, HD)

    stats = jnp.zeros((2 * tok, 128), F32)
    for ot in range(T):
        if ot:
            arrived(q, qar_sem.at[ot])
            arrived(go, gar_sem.at[ot])
        tt = lax.rem(t + T - ot, T)
        for h in range(heads):
            g = tt * heads + h
            cols = pl.ds(pl.multiple_of(g * HD, HD), HD)
            at = pl.ds(h * HD, HD)
            keys, values = kv_rows(0, cols), kv_rows(1, cols)
            scores = dot_t(qa[ot, :, at], keys) * scale
            top = jnp.max(scores, axis=-1, keepdims=True)
            e = jnp.exp(scores - top) * times
            gprob = dot_t(ga[ot, :, at], values)
            obuf[g] = jnp.dot(e[:tok].astype(BF16), values, preferred_element_type=F32)
            ebuf[g] = e[tok:]
            gbuf[g] = gprob
            mass = jnp.sum(e, axis=-1, keepdims=True)
            delta = jnp.sum(e[tok:] * gprob, axis=-1, keepdims=True)
            delta = jnp.concatenate([jnp.zeros_like(delta), delta], axis=0)
            top = jnp.where(times > 0.0, top, -1e30)
            stats = jnp.where(lane == g, top, stats)
            stats = jnp.where(lane == g + H, mass, stats)
            stats = jnp.where(lane == g + 2 * H, delta, stats)
    st[...] = stats
    for ot in range(1, T):
        send(st, sr.at[ot - 1], sts_sem.at[ot], str_sem.at[ot], dev(0, ot))
    for ot in range(1, T):
        arrived(st, str_sem.at[ot])
    every = [stats] + [sr[ot - 1] for ot in range(1, T)]
    top = every[0][:, :H]
    for v in every[1:]:
        top = jnp.maximum(top, v[:, :H])
    mass = jnp.zeros((2 * tok, H), F32)
    delta = jnp.zeros((2 * tok, H), F32)
    for v in every:
        weight = jnp.exp(v[:, :H] - top)
        mass = mass + weight * v[:, H:2 * H]
        delta = delta + weight * v[:, 2 * H:3 * H]
    alpha = jnp.exp(stats[:, :H] - top) / mass
    delta = delta / mass

    def scatter(src, dst, e, ssem, rsem):
        send_or_keep(src.at[e], dst.at[t], ssem.at[e], rsem.at[t], (s, e, d), t == e)

    for e in range(T):
        for h in range(heads):
            g = e * heads + h
            obs[e, :, pl.ds(h * HD, HD)] = (obuf[g] * alpha[:tok, g:g + 1]).astype(BF16)
        scatter(obs, obr, e, obs_sem, obr_sem)
    for e in range(T):
        slot_of = lax.rem(t + T - e, T)
        for h in range(heads):
            g = e * heads + h
            cols, at = pl.ds(g * HD, HD), pl.ds(h * HD, HD)
            keys = kv_rows(0, cols)
            probs = ebuf[g] * alpha[tok:, g:g + 1]
            gv = dot_0(probs.astype(BF16), ga[slot_of, :, at])
            gs = probs * (gbuf[g] - delta[tok:, g:g + 1])
            scaled = (gs * scale).astype(BF16)
            gqs[e, :, at] = jnp.dot(scaled, keys, preferred_element_type=F32).astype(BF16)
            gk = dot_0(scaled, qa[slot_of, pl.ds(tok, tok), at])
            kvs[:, 0, :, cols] = gk.astype(BF16).reshape(S, RB, HD)
            kvs[:, 1, :, cols] = gv.astype(BF16).reshape(S, RB, HD)
        scatter(gqs, gqp, e, gqps_sem, gqpr_sem)
    for os in pairs:
        ss, _, _ = dev(os)
        send(kvs.at[ss], kvg_ref.at[s], kgs_sem.at[os], kgr_sem.at[os], dev(os))
    keep_kvg = pltpu.make_async_copy(kvs.at[s], kvg_ref.at[s], kgr_sem.at[0])
    keep_kvg.start()

    half_scatter_wait(obr, obr_sem)
    total = obr[0].astype(F32)
    for e in range(1, T):
        total = total + obr[e].astype(F32)
    bl[...] = total.astype(BF16)
    half_gather(bl, blg, tok, bs_sem, br_sem)
    half_scatter_wait(gqp, gqpr_sem)
    total = gqp[0].astype(F32)
    for e in range(1, T):
        total = total + gqp[e].astype(F32)
    gqb[own] = total.astype(BF16)
    for od in range(1, N):
        send(gqb.at[own], gqb.at[own], gqs_sem.at[od], gqr_sem.at[od], dev(0, 0, od))
    row = jnp.sum(total * qf[...], axis=-1, keepdims=True)
    rts[...] = jnp.broadcast_to(row, rts.shape)
    for ot in range(1, T):
        send(rts, rtr.at[ot - 1], rs_sem.at[ot], rr_sem.at[ot], dev(0, ot, 0))

    for od in range(1, N):
        arrived(gqb.at[own], gqr_sem.at[od])
    for i in range(R):
        @pl.loop(0, W // TILE)
        def _(j):
            cols = pl.ds(pl.multiple_of(j * TILE, TILE), TILE)
            rows = pl.ds(pl.multiple_of(i * W + j * TILE, TILE), TILE)
            hs2[i, :, cols] = dot_t(gqb[...], wq[rows, :]).astype(BF16)
    half_scatter(hs2, hr2, h2s_sem, h2r_sem)

    half_gather_wait(blg, tok, br_sem)

    @pl.loop(0, W // TILE)
    def _(j):
        cols = pl.ds(pl.multiple_of(j * TILE, TILE), TILE)
        total = None
        for i in range(R):
            term = jnp.dot(blg[i], wo[pl.ds(i * W, W), cols], preferred_element_type=F32)
            total = term if total is None else total + term
        pp[:, cols] = total

    for od in range(1, N):
        e = lax.rem(d + od, N)
        send(pp.at[group(e, tok)], ppr.at[od - 1], pps_sem.at[od], ppr_sem.at[od], (s, t, e))
    total = fwd_ref[...].astype(F32) + pp[own]
    for od in range(1, N):
        arrived(ppr.at[od - 1], ppr_sem.at[od])
        total = total + ppr[od - 1]
    ns[...] = total.astype(BF16)
    send(ns, nr, sec_sem.at[0], sec_sem.at[1], dev(1))

    for ot in range(1, T):
        arrived(rtr.at[ot - 1], rr_sem.at[ot])
        row = row + rtr[ot - 1][:, :1]
    half_scatter_wait(hr2, h2r_sem)
    gn = hr2[0].astype(F32)
    for e in range(1, T):
        gn = gn + hr2[e].astype(F32)
    back = back_ref[...].astype(F32)
    gains = gain_ref[:, pl.ds(pl.multiple_of(t * W, W), W)]
    gp[...] = jnp.sum(gn * back * inv_back, axis=0, keepdims=True)
    for od in range(1, N):
        send(gp, gpr.at[od - 1], gps_sem.at[od], gpr_sem.at[od], dev(0, 0, od))
    wide = grad_ref[...].astype(F32) + gains * inv_back * gn
    wide = wide - back * (inv_back * inv_back * inv_back * row * (1.0 / width))
    ps[...] = wide.astype(BF16)
    send(ps, pr, sec_sem.at[2], sec_sem.at[3], dev(S - 1))
    total = gp[...]
    for od in range(1, N):
        arrived(gpr.at[od - 1], gpr_sem.at[od])
        total = total + gpr[od - 1]
    gg_ref[...] = total
    arrived(nr, sec_sem.at[1])
    next_ref[...] = nr[...]
    arrived(pr, sec_sem.at[3])
    keep = jnp.where(s < S - 1, 1.0, 0.0).astype(F32)
    prev_ref[...] = (pr[...].astype(F32) * keep).astype(BF16)
    keep_kvg.wait()
    for os in pairs:
        arrived(kvs.at[0], kgr_sem.at[os])
    for cond, copy in sent:
        if cond is None:
            copy.wait_send()
        else:
            pl.when(cond)(copy.wait_send)


def on_device(S, T, N, fwd_in, back_in, back_grad, gain, w_query, w_out, neighbour_kv, pattern):
    _, tok, W = fwd_in.shape
    rb = neighbour_kv.shape[1]
    D = gain.shape[1]
    half = w_query.shape[1]
    R = T // N
    H = D // HD
    kv = neighbour_kv.transpose(0, 2, 1, 3)
    picks = pattern.reshape(4)
    vm = pl.BlockSpec(memory_space=pltpu.VMEM)
    sm = pl.BlockSpec(memory_space=pltpu.SMEM)
    hb = pl.BlockSpec(memory_space=pl.ANY)
    V = pltpu.VMEM
    dma = lambda *n: pltpu.SemaphoreType.DMA(n)
    M = max(N - 1, 1)
    scratch = [
        V((half, W), BF16), V((half, W), BF16),
        V((2 * tok, W), BF16), V((R, N * 2 * tok, W), BF16), V((N * tok, W), BF16),
        V((S, 2, rb, D), BF16), V((S, 2, rb, D), BF16),
        V((R, N * tok, W), BF16), V((T, tok, W), BF16),
        V((N * 2 * tok, W), F32), V((M, 2 * tok, W), F32),
        V((N * 2 * tok, 128), F32), V((M, 2 * tok, 128), F32),
        V((2 * tok, W), BF16), V((tok, W), F32), V((tok, W), BF16),
        V((tok, W), BF16), V((R, N * tok, W), BF16), V((N * tok, W), BF16),
        V((tok, 128), F32), V((T - 1, tok, 128), F32),
        V((R, N * tok, W), BF16), V((T, tok, W), BF16),
        V((T, 2 * tok, W), BF16), V((T, tok, W), BF16),
        V((H, tok, S * rb), F32), V((H, tok, S * rb), F32), V((H, tok, HD), F32),
        V((2 * tok, 128), F32), V((T - 1, 2 * tok, 128), F32),
        V((T, tok, W), BF16), V((T, tok, W), BF16), V((T, tok, W), BF16), V((T, tok, W), BF16),
        V((N * tok, W), F32), V((M, tok, W), F32),
        V((1, W), F32), V((M, 1, W), F32),
        V((tok, W), BF16), V((tok, W), BF16), V((tok, W), BF16), V((tok, W), BF16),
        dma(2), dma(T), dma(R * N), dma(N), dma(N), dma(S), dma(S), dma(R * N), dma(T),
        dma(N), dma(N), dma(N), dma(N), dma(T), dma(R * N), dma(N), dma(N), dma(T), dma(T),
        dma(R * N), dma(T), dma(S), dma(S), dma(N), dma(N), dma(N), dma(N), dma(4),
        dma(T), dma(T), dma(T), dma(T), dma(T), dma(T), dma(T), dma(T), dma(T), dma(T),
    ]
    next_in, prev_grad, kvg, gg = pl.pallas_call(
        functools.partial(kernel, S, T, N),
        out_shape=[
            jax.ShapeDtypeStruct((tok, W), BF16),
            jax.ShapeDtypeStruct((tok, W), BF16),
            jax.ShapeDtypeStruct((S, 2, rb, D), BF16),
            jax.ShapeDtypeStruct((1, W), F32),
        ],
        in_specs=[sm, vm, vm, vm, vm, hb, hb, hb],
        out_specs=[vm, vm, hb, vm],
        scratch_shapes=scratch,
        compiler_params=pltpu.CompilerParams(
            collective_id=0, has_side_effects=True, vmem_limit_bytes=48 * 2**20
        ),
        cost_estimate=pl.CostEstimate(
            flops=5 * 10**9, bytes_accessed=14 * 2**20, transcendentals=2 * 10**5
        ),
    )(picks, fwd_in[0], back_in[0], back_grad[0], gain, w_query[0], w_out[0], kv)
    kv_grad = kvg.transpose(0, 2, 1, 3)
    return (next_in[None], prev_grad[None], kv_grad, gg)


def solution(mesh):
    S, T, N = (mesh.shape[a] for a in ("section", "tensor", "dp"))
    return jax.shard_map(
        functools.partial(on_device, S, T, N),
        mesh=mesh,
        in_specs=(
            P("section", "dp", "tensor"),
            P("section", "dp", "tensor"),
            P("section", "dp", "tensor"),
            P("section", None),
            P("section", "dp", "tensor"),
            P("section", "dp", "tensor"),
            P(None, ("section", "tensor", "dp"), None, None),
            P(None, "dp", None),
        ),
        out_specs=(
            P("section", "dp", "tensor"),
            P("section", "dp", "tensor"),
            P(None, ("section", "tensor", "dp"), None, None),
            P("section", "tensor"),
        ),
        check_vma=False,
    )
```

```python
import functools

import jax
import jax.numpy as jnp
from jax import lax
from jax.experimental import pallas as pl
from jax.experimental.pallas import tpu as pltpu
from jax.sharding import PartitionSpec as P

HD = 128
NBLK = 4
norm_eps = 1e-05
MESH = pl.DeviceIdType.MESH
F32 = jnp.float32
BF16 = jnp.bfloat16
TILE = 256


def dot_t(a, b):
    return lax.dot_general(a, b, (((1,), (1,)), ((), ())), preferred_element_type=F32)


def dot_0(a, b):
    return lax.dot_general(a, b, (((0,), (0,)), ((), ())), preferred_element_type=F32)


def kernel(
    S, T, N,
    pat_ref, fwd_ref, back_ref, grad_ref, gain_ref, wq_hbm, wo_hbm, kv_hbm,
    next_ref, prev_ref, kvg_ref, gg_ref,
    wq, wo, x, xg, hg, bgb, kvb, kvs, hs1, hr1, qp, qr, ssp, ssr, q, qf, go,
    bl, blg, gqb, rts, rtr, hs2, hr2, qa, ga, ebuf, gbuf, obuf, st, sr, obs, obr, gqs, gqp, pp, ppr, gp, gpr, ns, nr, ps, pr,
    w_sem, xs_sem, xr_sem, gs_sem, gr_sem, ks_sem, kr_sem, h1s_sem, h1r_sem,
    qs_sem, qr_sem, zs_sem, zr_sem, bs_sem, br_sem, gqs_sem, gqr_sem, rs_sem, rr_sem,
    h2s_sem, h2r_sem, kgs_sem, kgr_sem, pps_sem, ppr_sem, gps_sem, gpr_sem, sec_sem,
    qas_sem, qar_sem, gas_sem, gar_sem, sts_sem, str_sem, obs_sem, obr_sem, gqps_sem, gqpr_sem,
):
    s, t, d = lax.axis_index("section"), lax.axis_index("tensor"), lax.axis_index("dp")
    tok, W = fwd_ref.shape
    R = T // N
    RB = kv_hbm.shape[2]
    heads = W // HD
    H = T * heads
    rows_here = S * RB
    width = T * W

    def dev(os=0, ot=0, od=0):
        return (lax.rem(s + os, S), lax.rem(t + ot, T), lax.rem(d + od, N))

    pairs = list(range(1, S))
    others = [(ot, od) for ot in range(T) for od in range(N) if (ot, od) != (0, 0)]
    barrier = pltpu.get_barrier_semaphore()
    for os in pairs:
        pl.semaphore_signal(barrier, inc=1, device_id=dev(os), device_id_type=MESH)
    for ot, od in others:
        pl.semaphore_signal(barrier, inc=1, device_id=dev(0, ot, od), device_id_type=MESH)

    wo_copy = pltpu.make_async_copy(wo_hbm, wo, w_sem.at[0])
    wq_copy = pltpu.make_async_copy(wq_hbm, wq, w_sem.at[1])
    wo_copy.start()
    wq_copy.start()
    x[pl.ds(0, tok)] = fwd_ref[...]
    x[pl.ds(tok, tok)] = back_ref[...]
    own = pl.ds(pl.multiple_of(d * tok, tok), tok)
    bgb[own] = grad_ref[...]
    pl.semaphore_wait(barrier, len(pairs) + len(others))

    sent = []

    def send(src, dst, ssem, rsem, device):
        copy = pltpu.make_async_remote_copy(
            src_ref=src, dst_ref=dst, send_sem=ssem, recv_sem=rsem,
            device_id=device, device_id_type=MESH,
        )
        copy.start()
        sent.append((None, copy))

    def send_or_keep(src, dst, ssem, rsem, device, here):
        copy = pltpu.make_async_remote_copy(
            src_ref=src, dst_ref=dst, send_sem=ssem, recv_sem=rsem,
            device_id=device, device_id_type=MESH,
        )

        @pl.when(here)
        def _():
            pltpu.make_async_copy(src, dst, rsem).start()

        @pl.when(jnp.logical_not(here))
        def _():
            copy.start()

        sent.append((jnp.logical_not(here), copy))

    def send_if(cond, src, dst, ssem, rsem, device):
        copy = pltpu.make_async_remote_copy(
            src_ref=src, dst_ref=dst, send_sem=ssem, recv_sem=rsem,
            device_id=device, device_id_type=MESH,
        )
        pl.when(cond)(copy.start)
        sent.append((cond, copy))

    relay = T == 4 and N == 2

    def direct(ot):
        ends = jnp.logical_or(
            jnp.logical_and(t == 0, ot == T - 1), jnp.logical_and(t == T - 1, ot == 1)
        )
        return jnp.logical_not(ends)

    def arrived(ref, sem):
        pltpu.make_async_copy(ref, ref, sem).wait()

    core = t // R
    part = lax.rem(t, R)
    slot = part * N + d

    def half_gather(src, dst, rows, ssem, rsem):
        at = pl.ds(pl.multiple_of(d * rows, rows), rows)
        for ot in range(T):
            tt = lax.rem(t + ot, T)
            device = (s, tt, core)
            if ot == 0:
                send_or_keep(src, dst.at[part, at], ssem.at[ot], rsem.at[slot], device, core == d)
            elif relay and ot != 2:
                send_if(direct(ot), src, dst.at[part, at], ssem.at[ot], rsem.at[slot], device)
            else:
                send(src, dst.at[part, at], ssem.at[ot], rsem.at[slot], device)

    def half_gather_wait(dst, rows, ssem, rsem):
        relayed = relay and N == 2
        order = [d, 1 - d] if relayed else list(range(R))
        for k, i in enumerate(order):
            for e in range(N):
                ref = dst.at[i, pl.ds(e * rows, rows)]
                arrived(ref, rsem.at[i * N + e])
                if relayed and k == 0:
                    send_if(
                        t == 2 - d, ref, ref, ssem.at[T + e], rsem.at[i * N + e],
                        (s, 3 * (1 - d), d),
                    )

    def half_scatter(src, dst, ssem, rsem):
        for i in range(R):
            for e in range(N):
                here = jnp.logical_and(R * d + i == t, d == e)
                send_or_keep(
                    src.at[i, pl.ds(e * tok, tok)], dst.at[t], ssem.at[i * N + e],
                    rsem.at[t], (s, R * d + i, e), here,
                )

    def half_scatter_wait(dst, rsem):
        for e in range(T):
            arrived(dst.at[e], rsem.at[e])

    half_gather(x, xg, 2 * tok, xs_sem, xr_sem)
    for od in range(1, N):
        send(grad_ref, bgb.at[own], gs_sem.at[od], gr_sem.at[od], dev(0, 0, od))
    for os in pairs:
        ss, _, _ = dev(os)
        send(kv_hbm.at[ss], kvb.at[s], ks_sem.at[os], kr_sem.at[os], dev(os))
    keep_kv = pltpu.make_async_copy(kv_hbm.at[s], kvb.at[s], kr_sem.at[0])
    keep_kv.start()

    for od in range(1, N):
        arrived(bgb.at[own], gr_sem.at[od])
    wo_copy.wait()
    for i in range(R):
        @pl.loop(0, W // TILE)
        def _(j):
            cols = pl.ds(pl.multiple_of(j * TILE, TILE), TILE)
            rows = pl.ds(pl.multiple_of(i * W + j * TILE, TILE), TILE)
            hs1[i, :, cols] = dot_t(bgb[...], wo[rows, :]).astype(BF16)
    half_scatter(hs1, hr1, h1s_sem, h1r_sem)

    wq_copy.wait()
    half_gather_wait(xg, 2 * tok, xs_sem, xr_sem)
    squares = None
    for i in range(R):
        wide = xg[i].astype(F32)
        term = jnp.sum(wide * wide, axis=-1, keepdims=True)
        squares = term if squares is None else squares + term
        gains = gain_ref[:, pl.ds(pl.multiple_of((d * R + i) * W, W), W)]
        hg[i] = (wide * gains).astype(BF16)
    ssp[...] = jnp.broadcast_to(squares, ssp.shape)

    @pl.loop(0, W // TILE)
    def _(j):
        cols = pl.ds(pl.multiple_of(j * TILE, TILE), TILE)
        total = None
        for i in range(R):
            term = jnp.dot(hg[i], wq[pl.ds(i * W, W), cols], preferred_element_type=F32)
            total = term if total is None else total + term
        qp[:, cols] = total

    def group(e, rows):
        return pl.ds(pl.multiple_of(e * rows, rows), rows)

    for od in range(1, N):
        e = lax.rem(d + od, N)
        send(qp.at[group(e, 2 * tok)], qr.at[od - 1], qs_sem.at[od], qr_sem.at[od], (s, t, e))
        send(ssp.at[group(e, 2 * tok)], ssr.at[od - 1], zs_sem.at[od], zr_sem.at[od], (s, t, e))
    total = qp[group(d, 2 * tok)]
    squares = ssp[group(d, 2 * tok)]
    for od in range(1, N):
        arrived(qr.at[od - 1], qr_sem.at[od])
        arrived(ssr.at[od - 1], zr_sem.at[od])
        total = total + qr[od - 1]
        squares = squares + ssr[od - 1]
    inv = lax.rsqrt(squares[:, :1] * (1.0 / width) + norm_eps)
    q[...] = (total * inv).astype(BF16)
    qf[...] = total[tok:]
    inv_back = inv[tok:]
    def gather_send(src, dst, ot, ssem, rsem):
        if relay and ot != 2:
            send_if(direct(ot), src, dst.at[ot], ssem.at[ot], rsem.at[ot], dev(0, ot))
        else:
            send(src, dst.at[ot], ssem.at[ot], rsem.at[ot], dev(0, ot))

    def gather_wait(dst, ot, ssem, rsem):
        arrived(dst.at[ot], rsem.at[ot])
        if relay and ot == 2:
            to = jnp.where(t == 2, 3, 1)
            send_if(
                jnp.logical_or(t == 1, t == 2), dst.at[2], dst.at[to], ssem.at[0],
                rsem.at[to], (s, jnp.where(t == 2, 3, 0), d),
            )

    qa[0] = q[...]
    for ot in range(1, T):
        gather_send(q, qa, ot, qas_sem, qar_sem)
    half_scatter_wait(hr1, h1r_sem)
    total = hr1[0].astype(F32)
    for e in range(1, T):
        total = total + hr1[e].astype(F32)
    go[...] = total.astype(BF16)
    ga[0] = go[...]
    for ot in range(1, T):
        gather_send(go, ga, ot, gas_sem, gar_sem)

    scale = HD ** (-0.5)
    block = t * NBLK // T
    counts = []
    for m in range(2):
        count = jnp.float32(0.0)
        for j in range(2):
            count = count + jnp.where(pat_ref[m, 0, j] == block, 1.0, 0.0).astype(F32)
        counts.append(count)
    is_fwd = lax.broadcasted_iota(jnp.int32, (2 * tok, 1), 0) < tok
    times = jnp.where(is_fwd, counts[0], counts[1])
    lane = lax.broadcasted_iota(jnp.int32, (2 * tok, 128), 1)
    keep_kv.wait()
    for os in pairs:
        arrived(kvb.at[s], kr_sem.at[os])

    def kv_rows(kind, cols):
        return kvb[:, kind, :, cols].reshape(rows_here, HD)

    stats = jnp.zeros((2 * tok, 128), F32)
    for ot in [0, 2, 1, 3] if relay else range(T):
        if ot:
            gather_wait(qa, ot, qas_sem, qar_sem)
            gather_wait(ga, ot, gas_sem, gar_sem)
        tt = lax.rem(t + T - ot, T)
        for h in range(heads):
            g = tt * heads + h
            cols = pl.ds(pl.multiple_of(g * HD, HD), HD)
            at = pl.ds(h * HD, HD)
            keys, values = kv_rows(0, cols), kv_rows(1, cols)
            scores = dot_t(qa[ot, :, at], keys) * scale
            top = jnp.max(scores, axis=-1, keepdims=True)
            e = jnp.exp(scores - top) * times
            gprob = dot_t(ga[ot, :, at], values)
            obuf[g] = jnp.dot(e[:tok].astype(BF16), values, preferred_element_type=F32)
            ebuf[g] = e[tok:]
            gbuf[g] = gprob
            mass = jnp.sum(e, axis=-1, keepdims=True)
            delta = jnp.sum(e[tok:] * gprob, axis=-1, keepdims=True)
            delta = jnp.concatenate([jnp.zeros_like(delta), delta], axis=0)
            top = jnp.where(times > 0.0, top, -1e30)
            stats = jnp.where(lane == g, top, stats)
            stats = jnp.where(lane == g + H, mass, stats)
            stats = jnp.where(lane == g + 2 * H, delta, stats)
    st[...] = stats
    for ot in range(1, T):
        send(st, sr.at[ot - 1], sts_sem.at[ot], str_sem.at[ot], dev(0, ot))
    for ot in range(1, T):
        arrived(st, str_sem.at[ot])
    every = [stats] + [sr[ot - 1] for ot in range(1, T)]
    top = every[0][:, :H]
    for v in every[1:]:
        top = jnp.maximum(top, v[:, :H])
    mass = jnp.zeros((2 * tok, H), F32)
    delta = jnp.zeros((2 * tok, H), F32)
    for v in every:
        weight = jnp.exp(v[:, :H] - top)
        mass = mass + weight * v[:, H:2 * H]
        delta = delta + weight * v[:, 2 * H:3 * H]
    alpha = jnp.exp(stats[:, :H] - top) / mass
    delta = delta / mass

    def scatter(src, dst, e, ssem, rsem):
        send_or_keep(src.at[e], dst.at[t], ssem.at[e], rsem.at[t], (s, e, d), t == e)

    for e in range(T):
        for h in range(heads):
            g = e * heads + h
            obs[e, :, pl.ds(h * HD, HD)] = (obuf[g] * alpha[:tok, g:g + 1]).astype(BF16)
        scatter(obs, obr, e, obs_sem, obr_sem)
    for e in range(T):
        slot_of = lax.rem(t + T - e, T)
        for h in range(heads):
            g = e * heads + h
            cols, at = pl.ds(g * HD, HD), pl.ds(h * HD, HD)
            keys = kv_rows(0, cols)
            probs = ebuf[g] * alpha[tok:, g:g + 1]
            gv = dot_0(probs.astype(BF16), ga[slot_of, :, at])
            gs = probs * (gbuf[g] - delta[tok:, g:g + 1])
            scaled = (gs * scale).astype(BF16)
            gqs[e, :, at] = jnp.dot(scaled, keys, preferred_element_type=F32).astype(BF16)
            gk = dot_0(scaled, qa[slot_of, pl.ds(tok, tok), at])
            kvs[:, 0, :, cols] = gk.astype(BF16).reshape(S, RB, HD)
            kvs[:, 1, :, cols] = gv.astype(BF16).reshape(S, RB, HD)
        scatter(gqs, gqp, e, gqps_sem, gqpr_sem)
    for os in pairs:
        ss, _, _ = dev(os)
        send(kvs.at[ss], kvg_ref.at[s], kgs_sem.at[os], kgr_sem.at[os], dev(os))
    keep_kvg = pltpu.make_async_copy(kvs.at[s], kvg_ref.at[s], kgr_sem.at[0])
    keep_kvg.start()

    half_scatter_wait(obr, obr_sem)
    total = obr[0].astype(F32)
    for e in range(1, T):
        total = total + obr[e].astype(F32)
    bl[...] = total.astype(BF16)
    half_gather(bl, blg, tok, bs_sem, br_sem)
    half_scatter_wait(gqp, gqpr_sem)
    total = gqp[0].astype(F32)
    for e in range(1, T):
        total = total + gqp[e].astype(F32)
    gqb[own] = total.astype(BF16)
    for od in range(1, N):
        send(gqb.at[own], gqb.at[own], gqs_sem.at[od], gqr_sem.at[od], dev(0, 0, od))
    row = jnp.sum(total * qf[...], axis=-1, keepdims=True)
    rts[...] = jnp.broadcast_to(row, rts.shape)
    for ot in range(1, T):
        send(rts, rtr.at[ot - 1], rs_sem.at[ot], rr_sem.at[ot], dev(0, ot, 0))

    for od in range(1, N):
        arrived(gqb.at[own], gqr_sem.at[od])
    for i in range(R):
        @pl.loop(0, W // TILE)
        def _(j):
            cols = pl.ds(pl.multiple_of(j * TILE, TILE), TILE)
            rows = pl.ds(pl.multiple_of(i * W + j * TILE, TILE), TILE)
            hs2[i, :, cols] = dot_t(gqb[...], wq[rows, :]).astype(BF16)
    half_scatter(hs2, hr2, h2s_sem, h2r_sem)

    half_gather_wait(blg, tok, bs_sem, br_sem)

    @pl.loop(0, W // TILE)
    def _(j):
        cols = pl.ds(pl.multiple_of(j * TILE, TILE), TILE)
        total = None
        for i in range(R):
            term = jnp.dot(blg[i], wo[pl.ds(i * W, W), cols], preferred_element_type=F32)
            total = term if total is None else total + term
        pp[:, cols] = total

    for od in range(1, N):
        e = lax.rem(d + od, N)
        send(pp.at[group(e, tok)], ppr.at[od - 1], pps_sem.at[od], ppr_sem.at[od], (s, t, e))
    total = fwd_ref[...].astype(F32) + pp[own]
    for od in range(1, N):
        arrived(ppr.at[od - 1], ppr_sem.at[od])
        total = total + ppr[od - 1]
    ns[...] = total.astype(BF16)
    send(ns, nr, sec_sem.at[0], sec_sem.at[1], dev(1))

    for ot in range(1, T):
        arrived(rtr.at[ot - 1], rr_sem.at[ot])
        row = row + rtr[ot - 1][:, :1]
    half_scatter_wait(hr2, h2r_sem)
    gn = hr2[0].astype(F32)
    for e in range(1, T):
        gn = gn + hr2[e].astype(F32)
    back = back_ref[...].astype(F32)
    gains = gain_ref[:, pl.ds(pl.multiple_of(t * W, W), W)]
    gp[...] = jnp.sum(gn * back * inv_back, axis=0, keepdims=True)
    for od in range(1, N):
        send(gp, gpr.at[od - 1], gps_sem.at[od], gpr_sem.at[od], dev(0, 0, od))
    wide = grad_ref[...].astype(F32) + gains * inv_back * gn
    wide = wide - back * (inv_back * inv_back * inv_back * row * (1.0 / width))
    ps[...] = wide.astype(BF16)
    send(ps, pr, sec_sem.at[2], sec_sem.at[3], dev(S - 1))
    total = gp[...]
    for od in range(1, N):
        arrived(gpr.at[od - 1], gpr_sem.at[od])
        total = total + gpr[od - 1]
    gg_ref[...] = total
    arrived(nr, sec_sem.at[1])
    next_ref[...] = nr[...]
    arrived(pr, sec_sem.at[3])
    keep = jnp.where(s < S - 1, 1.0, 0.0).astype(F32)
    prev_ref[...] = (pr[...].astype(F32) * keep).astype(BF16)
    keep_kvg.wait()
    for os in pairs:
        arrived(kvs.at[0], kgr_sem.at[os])
    for cond, copy in sent:
        if cond is None:
            copy.wait_send()
        else:
            pl.when(cond)(copy.wait_send)


def on_device(S, T, N, fwd_in, back_in, back_grad, gain, w_query, w_out, neighbour_kv, pattern):
    _, tok, W = fwd_in.shape
    rb = neighbour_kv.shape[1]
    D = gain.shape[1]
    half = w_query.shape[1]
    R = T // N
    H = D // HD
    kv = neighbour_kv.transpose(0, 2, 1, 3)
    vm = pl.BlockSpec(memory_space=pltpu.VMEM)
    sm = pl.BlockSpec(memory_space=pltpu.SMEM)
    hb = pl.BlockSpec(memory_space=pl.ANY)
    V = pltpu.VMEM
    dma = lambda *n: pltpu.SemaphoreType.DMA(n)
    M = max(N - 1, 1)
    scratch = [
        V((half, W), BF16), V((half, W), BF16),
        V((2 * tok, W), BF16), V((R, N * 2 * tok, W), BF16), V((R, N * 2 * tok, W), BF16),
        V((N * tok, W), BF16),
        V((S, 2, rb, D), BF16), V((S, 2, rb, D), BF16),
        V((R, N * tok, W), BF16), V((T, tok, W), BF16),
        V((N * 2 * tok, W), F32), V((M, 2 * tok, W), F32),
        V((N * 2 * tok, 128), F32), V((M, 2 * tok, 128), F32),
        V((2 * tok, W), BF16), V((tok, W), F32), V((tok, W), BF16),
        V((tok, W), BF16), V((R, N * tok, W), BF16), V((N * tok, W), BF16),
        V((tok, 128), F32), V((T - 1, tok, 128), F32),
        V((R, N * tok, W), BF16), V((T, tok, W), BF16),
        V((T, 2 * tok, W), BF16), V((T, tok, W), BF16),
        V((H, tok, S * rb), F32), V((H, tok, S * rb), F32), V((H, tok, HD), F32),
        V((2 * tok, 128), F32), V((T - 1, 2 * tok, 128), F32),
        V((T, tok, W), BF16), V((T, tok, W), BF16), V((T, tok, W), BF16), V((T, tok, W), BF16),
        V((N * tok, W), F32), V((M, tok, W), F32),
        V((1, W), F32), V((M, 1, W), F32),
        V((tok, W), BF16), V((tok, W), BF16), V((tok, W), BF16), V((tok, W), BF16),
        dma(2), dma(T + N), dma(R * N), dma(N), dma(N), dma(S), dma(S), dma(R * N), dma(T),
        dma(N), dma(N), dma(N), dma(N), dma(T + N), dma(R * N), dma(N), dma(N), dma(T), dma(T),
        dma(R * N), dma(T), dma(S), dma(S), dma(N), dma(N), dma(N), dma(N), dma(4),
        dma(T), dma(T), dma(T), dma(T), dma(T), dma(T), dma(T), dma(T), dma(T), dma(T),
    ]
    next_in, prev_grad, kvg, gg = pl.pallas_call(
        functools.partial(kernel, S, T, N),
        out_shape=[
            jax.ShapeDtypeStruct((tok, W), BF16),
            jax.ShapeDtypeStruct((tok, W), BF16),
            jax.ShapeDtypeStruct((S, 2, rb, D), BF16),
            jax.ShapeDtypeStruct((1, W), F32),
        ],
        in_specs=[sm, vm, vm, vm, vm, hb, hb, hb],
        out_specs=[vm, vm, hb, vm],
        scratch_shapes=scratch,
        compiler_params=pltpu.CompilerParams(
            collective_id=0, has_side_effects=True, vmem_limit_bytes=48 * 2**20
        ),
        cost_estimate=pl.CostEstimate(
            flops=5 * 10**9, bytes_accessed=14 * 2**20, transcendentals=2 * 10**5
        ),
    )(pattern, fwd_in[0], back_in[0], back_grad[0], gain, w_query[0], w_out[0], kv)
    kv_grad = kvg.transpose(0, 2, 1, 3)
    return (next_in[None], prev_grad[None], kv_grad, gg)


def solution(mesh):
    S, T, N = (mesh.shape[a] for a in ("section", "tensor", "dp"))
    return jax.shard_map(
        functools.partial(on_device, S, T, N),
        mesh=mesh,
        in_specs=(
            P("section", "dp", "tensor"),
            P("section", "dp", "tensor"),
            P("section", "dp", "tensor"),
            P("section", None),
            P("section", "dp", "tensor"),
            P("section", "dp", "tensor"),
            P(None, ("section", "tensor", "dp"), None, None),
            P(None, "dp", None),
        ),
        out_specs=(
            P("section", "dp", "tensor"),
            P("section", "dp", "tensor"),
            P(None, ("section", "tensor", "dp"), None, None),
            P("section", "tensor"),
        ),
        check_vma=False,
    )
```
